32 devices in a mesh: seq: 8 (over y, x, core), dp: 4 (over z).
Axes of the slice: x: 2, y: 2, z: 4, core: 2. Of those that a mesh axis runs over, the one named last changes fastest.
Arguments:
- normed_input: bfloat16 [4, 1024, 5376], P('dp', 'seq'), may hold values from -6 to 6
- q_base: bfloat16 [4, 1024, 2048], P('dp', 'seq'), may hold values from -6 to 6
- k_base: bfloat16 [4, 1024, 1024], P('dp', 'seq'), may hold values from -6 to 6
- v_base: bfloat16 [4, 1024, 1024], P('dp', 'seq'), may hold values from -6 to 6
- d_attn: bfloat16 [4, 1024, 2048], P('dp', 'seq'), may hold values from -0.09375 to 0.09375
- lengths: int32 [4], P('dp'), may hold values from 512 to 1024
- a_query: bfloat16 [5376, 16], replicated, may hold values from -0.078125 to 0.078125
- b_query: bfloat16 [16, 2048], replicated, may hold values from -0.8984375 to 0.8984375
- a_key: bfloat16 [5376, 16], replicated, may hold values from -0.078125 to 0.078125
- b_key: bfloat16 [16, 1024], replicated, may hold values from -0.8984375 to 0.8984375
- a_value: bfloat16 [5376, 16], replicated, may hold values from -0.078125 to 0.078125
- b_value: bfloat16 [16, 1024], replicated, may hold values from -0.8984375 to 0.8984375
Outputs:
- attention: bfloat16 [4, 1024, 2048], P('dp', 'seq')
- grad_a_query: float32 [5376, 16], replicated
- grad_b_query: float32 [16, 2048], replicated
- grad_a_key: float32 [5376, 16], replicated
- grad_b_key: float32 [16, 1024], replicated
- grad_a_value: float32 [5376, 16], replicated
- grad_b_value: float32 [16, 1024], replicated
The draws below stay inside these ranges and needn't reach their ends.
All inputs are finite; a program needn't handle non-finite values.
Results may differ from the reference program's by a relative error of at most 0.006.
The reference program's roundings to bfloat16 on the way (of `probs_low`, `d_out` and `dscore`) count: a program that leaves them out, or rounds other values in their place, can miss the bound.
Values may be sent and summed in bfloat16 or wider, within the bound.
A program may use at most 64 MiB of HBM per device.

```python
import jax
import jax.numpy as jnp
from jax import lax

D = 5376
HD = 128
HQ = 16
HK = 8
RANK = 16
WINDOW = 384
TOK_DEV = 128
HOPS = 3
SEQ = 1024
FILINGS = 4
TOKENS = 4096


def paired_fields(key):
    query_key = jax.random.fold_in(key, 101)
    keyset_key = jax.random.fold_in(key, 202)
    query_shape = (FILINGS, SEQ, HK, 2, HD)
    keyset_shape = (FILINGS, SEQ, HK, HD)
    query = jnp.clip(jax.random.normal(query_key, query_shape, jnp.float32), -6.0, 6.0)
    keyset = jnp.clip(jax.random.normal(keyset_key, keyset_shape, jnp.float32), -6.0, 6.0)
    return (query.reshape(FILINGS, SEQ, HQ * HD), keyset.reshape(FILINGS, SEQ, HK * HD))


def draw_q_base(key, part):
    query, keyset = paired_fields(key)
    return query.astype(jnp.bfloat16)


def draw_k_base(key, part):
    query, keyset = paired_fields(key)
    return keyset.astype(jnp.bfloat16)


def plant(values, stream_key, low, largest):
    longest = values.shape.index(max(values.shape))
    spots = []
    for shift in (0, 1):
        where = [jax.random.randint(jax.random.fold_in(stream_key, axis), (), 0, length) for axis, length in enumerate(values.shape)]
        where[longest] = (where[longest] + shift) % values.shape[longest]
        spots.append(tuple(where))
    return values.at[spots[0]].set(low).at[spots[1]].set(largest)


def shard_levels(rng, dims, split, smallest, largest):
    gain, own = 1.0, jax.random.fold_in(rng, 6)
    for axis_at, parts in split:
        draws = jnp.exp(jax.random.uniform(jax.random.fold_in(own, axis_at), (parts,), jnp.float32, smallest / len(split), largest / len(split)))
        gain = gain * jnp.repeat(draws, dims[axis_at] // parts).reshape([-1 if axis == axis_at else 1 for axis in range(len(dims))])
    return gain


def normal_values(key, dims, width, most, split=(), held_as=jnp.bfloat16):
    result = jax.random.normal(key, dims, jnp.float32) * width
    if len(split) > 0:
        result = shard_levels(key, dims, split, -0.22, 0.18) * result
    return jnp.clip(result, min=-most, max=most).astype(held_as)


def setup_inputs(seed: int = 0) -> dict:
    keys = jax.random.split(jax.random.key(seed), 13)
    normed_input = normal_values(keys[0], (FILINGS, SEQ, D), 1.0, 6.0, ((0, 4), (1, 8)))
    q_base = draw_q_base(jax.random.fold_in(keys[12], 71), 0)
    k_base = draw_k_base(jax.random.fold_in(keys[12], 71), 0)
    v_base = normal_values(keys[3], (FILINGS, SEQ, HK * HD), 1.0, 6.0, ((0, 4), (1, 8)))
    d_attn = normal_values(keys[4], (FILINGS, SEQ, HQ * HD), (TOKENS ** -0.5), 0.09375, ((0, 4), (1, 8)))
    lengths = plant(jax.random.randint(keys[5], (FILINGS,), SEQ // 2, SEQ + 1), jax.random.fold_in(keys[5], 1), SEQ // 2, SEQ).astype(jnp.int32)
    a_query = normal_values(keys[6], (D, RANK), D ** -0.5, 0.078125)
    b_query = normal_values(keys[7], (RANK, HQ * HD), 0.15, 0.8984375)
    a_key = normal_values(keys[8], (D, RANK), D ** -0.5, 0.078125)
    b_key = normal_values(keys[9], (RANK, HK * HD), 0.15, 0.8984375)
    a_value = normal_values(keys[10], (D, RANK), D ** -0.5, 0.078125)
    b_value = normal_values(keys[11], (RANK, HK * HD), 0.15, 0.8984375)
    return dict(normed_input=normed_input, q_base=q_base, k_base=k_base, v_base=v_base, d_attn=d_attn, lengths=lengths, a_query=a_query, b_query=b_query, a_key=a_key, b_key=b_key, a_value=a_value, b_value=b_value)


attn_scale = 168.0 ** -0.5
mask_fill = -1e30


def attend(query, keyset, values, d_out, allowed):
    query = query.astype(jnp.float32)
    keyset = keyset.astype(jnp.float32)
    values = values.astype(jnp.float32)
    d_out = d_out.astype(jnp.float32)
    scores = jnp.einsum('qgrd,kgd->grqk', query, keyset) * attn_scale
    scores = jnp.where(allowed[None, None], scores, mask_fill)
    top_score = jnp.max(scores, axis=-1, keepdims=True)
    raw_weight = jnp.exp(scores - top_score)
    probs = raw_weight / jnp.sum(raw_weight, axis=-1, keepdims=True)
    probs_low = lax.optimization_barrier(probs.astype(jnp.bfloat16)).astype(jnp.float32)
    output = jnp.einsum('grqk,kgd->qgrd', probs_low, values)
    dprob = jnp.einsum('qgrd,kgd->grqk', d_out, values)
    delta = jnp.sum(probs * dprob, axis=-1, keepdims=True)
    dscore = lax.optimization_barrier((probs * (dprob - delta)).astype(jnp.bfloat16)).astype(jnp.float32)
    d_query = jnp.einsum('grqk,kgd->qgrd', dscore, keyset) * attn_scale
    d_key = jnp.einsum('grqk,qgrd->kgd', dscore, query) * attn_scale
    d_value = jnp.einsum('grqk,qgrd->kgd', probs_low, d_out)
    return output, d_query, d_key, d_value


def reference(normed_input, q_base, k_base, v_base, d_attn, lengths, a_query, b_query, a_key, b_key, a_value, b_value):
    def lowrank(rows, a_matrix):
        return jnp.dot(rows, a_matrix, preferred_element_type=jnp.float32).astype(jnp.bfloat16)

    def lifted(base, low, b_matrix):
        return (base.astype(jnp.float32) + jnp.dot(low, b_matrix, preferred_element_type=jnp.float32)).astype(jnp.bfloat16)

    def adapter_grads(rows, low, grad, b_matrix):
        u_term = jnp.dot(grad, b_matrix.astype(jnp.float32).T, precision=lax.Precision.HIGHEST).astype(jnp.bfloat16)
        grad_a = jnp.dot(rows.T, u_term, preferred_element_type=jnp.float32)
        grad_b = jnp.dot(low.astype(jnp.float32).T, grad, precision=lax.Precision.HIGHEST)
        return grad_a, grad_b

    pad_rows = HOPS * TOK_DEV

    def filing(inputs):
        rows, base_q, base_k, base_v, grad_out, length = inputs
        low_query = lowrank(rows, a_query)
        low_key = lowrank(rows, a_key)
        low_value = lowrank(rows, a_value)
        query = lifted(base_q, low_query, b_query)
        keyset = lifted(base_k, low_key, b_key)
        values = lifted(base_v, low_value, b_value)
        position = jnp.arange(SEQ, dtype=jnp.int32)
        live = position < length
        d_out = jnp.where(live[:, None], grad_out, jnp.zeros_like(grad_out))
        padding = jnp.zeros((pad_rows, HK * HD), keyset.dtype)
        key_pad = jnp.concatenate([padding, keyset], 0)
        value_pad = jnp.concatenate([padding, values], 0)
        span = pad_rows + TOK_DEV

        def step(carry, block):
            dkey_pad, dvalue_pad = carry
            start = (block * TOK_DEV).astype(jnp.int32)
            query_blk = lax.dynamic_slice_in_dim(query, start, TOK_DEV, 0)
            dout_blk = lax.dynamic_slice_in_dim(d_out, start, TOK_DEV, 0)
            key_blk = lax.dynamic_slice_in_dim(key_pad, start, span, 0)
            value_blk = lax.dynamic_slice_in_dim(value_pad, start, span, 0)
            query_pos = start + jnp.arange(TOK_DEV, dtype=jnp.int32)
            key_pos = start - pad_rows + jnp.arange(span, dtype=jnp.int32)
            offset = query_pos[:, None] - key_pos[None, :]
            allowed = (key_pos[None, :] >= 0) & (offset >= 0) & (offset <= WINDOW) & ((key_pos[None, :] < length) | (offset == 0))
            output, d_query, d_key, d_value = attend(
                query_blk.reshape(TOK_DEV, HK, 2, HD), key_blk.reshape(span, HK, HD),
                value_blk.reshape(span, HK, HD), dout_blk.reshape(TOK_DEV, HK, 2, HD), allowed)
            old_key = lax.dynamic_slice_in_dim(dkey_pad, start, span, 0)
            old_value = lax.dynamic_slice_in_dim(dvalue_pad, start, span, 0)
            dkey_pad = lax.dynamic_update_slice_in_dim(dkey_pad, old_key + d_key.reshape(span, HK * HD), start, 0)
            dvalue_pad = lax.dynamic_update_slice_in_dim(dvalue_pad, old_value + d_value.reshape(span, HK * HD), start, 0)
            return (dkey_pad, dvalue_pad), (output.reshape(TOK_DEV, HQ * HD), d_query.reshape(TOK_DEV, HQ * HD))

        empty = jnp.zeros((pad_rows + SEQ, HK * HD), jnp.float32)
        blocks = jnp.arange(SEQ // TOK_DEV, dtype=jnp.int32)
        (dkey_pad, dvalue_pad), (outputs, dqueries) = lax.scan(step, (empty, empty), blocks)
        attention = outputs.reshape(SEQ, HQ * HD)
        attention = jnp.where(live[:, None], attention, jnp.zeros_like(attention)).astype(jnp.bfloat16)
        d_query = dqueries.reshape(SEQ, HQ * HD)
        d_key = dkey_pad[pad_rows:]
        d_value = dvalue_pad[pad_rows:]
        gaq, gbq = adapter_grads(rows, low_query, d_query, b_query)
        gak, gbk = adapter_grads(rows, low_key, d_key, b_key)
        gav, gbv = adapter_grads(rows, low_value, d_value, b_value)
        return attention, (gaq, gbq, gak, gbk, gav, gbv)

    attention, grads = lax.map(filing, (normed_input, q_base, k_base, v_base, d_attn, lengths))
    summed = [jnp.sum(grad, axis=0) for grad in grads]
    return attention, summed[0], summed[1], summed[2], summed[3], summed[4], summed[5]
```

```python
import functools

import jax
import jax.numpy as jnp
from jax import lax
from jax.experimental import pallas as pl
from jax.experimental.pallas import tpu as pltpu
from jax.sharding import PartitionSpec as P

HD = 128
WINDOW = 384
HOPS = 3
LANES = 128

attn_scale = 168.0 ** (-0.5)
mask_fill = -1e30
f32 = jnp.float32
bf16 = jnp.bfloat16


def dot(left, right, left_dim, right_dim):
    return lax.dot_general(
        left, right, (((left_dim,), (right_dim,)), ((), ())), preferred_element_type=f32
    )


def halves(value):
    high = value.astype(bf16)
    return high, (value - high.astype(f32)).astype(bf16)


def remote(src, dst, send_sem, recv_sem, **device):
    return pltpu.make_async_remote_copy(
        src_ref=src,
        dst_ref=dst,
        send_sem=send_sem,
        recv_sem=recv_sem,
        device_id=device,
        device_id_type=pl.DeviceIdType.MESH,
    )


def kernel(
    n_seq,
    n_dp,
    per_piece,
    rows,
    q_base,
    k_base,
    v_base,
    d_attn,
    length_ref,
    a_query,
    a_key,
    a_value,
    b_query,
    b_key,
    b_value,
    attention,
    out_aq,
    out_bq,
    out_ak,
    out_bk,
    out_av,
    out_bv,
    qs,
    ds,
    kv,
    lows,
    bias,
    b2q,
    b2k,
    b2v,
    uq,
    ukv,
    u_came,
    gsum,
    core_in,
    chip_out,
    chip_in,
    dp_out,
    dp_in,
    final,
    kv_send,
    kv_recv,
    relay_send,
    low_send,
    low_recv,
    u_send,
    u_recv,
    s1_send,
    s1_recv,
    s2_send,
    s2_recv,
    s3_send,
    s3_recv,
    s4_send,
    s4_recv,
    s5_send,
    s5_recv,
    s6_send,
    s6_recv,
):
    tok = rows.shape[0]
    width = rows.shape[1]
    rank = b_query.shape[0]
    groups = k_base.shape[1] // HD
    chunks = groups // 2
    n_chip = n_seq // 2
    seq = lax.axis_index("seq")
    dp = lax.axis_index("dp")
    core = lax.rem(seq, 2)
    chip = seq // 2
    sibling = seq + 1 - 2 * core
    own = HOPS * tok
    span = own + tok

    barrier = pltpu.get_barrier_semaphore()
    offsets = {step % n_seq for hop in range(1, HOPS + 1) for step in (hop, -hop)}
    offsets |= set(range(2, n_seq, 2))
    offsets.discard(0)
    for offset in sorted(offsets):
        pl.semaphore_signal(
            barrier,
            inc=1,
            device_id={"seq": lax.rem(seq + offset, n_seq)},
            device_id_type=pl.DeviceIdType.MESH,
        )
    for offset in range(1, n_dp):
        pl.semaphore_signal(
            barrier,
            inc=1,
            device_id={"dp": lax.rem(dp + offset, n_dp)},
            device_id_type=pl.DeviceIdType.MESH,
        )

    joined = jnp.concatenate(
        [a_query[...], a_key[...], a_value[...], jnp.zeros((LANES - 3 * rank, width), bf16)], 0
    )
    low = dot(rows[...], joined, 1, 1)
    low_t = jnp.transpose(low.astype(bf16).astype(f32)).astype(bf16)
    lowq_t = low_t[:rank]
    lowk_t = low_t[rank : 2 * rank]
    lowv_t = low_t[2 * rank : 3 * rank]
    lows[HOPS] = low_t[rank : 3 * rank]
    for chunk in range(chunks):
        cols = slice(chunk * 2 * HD, (chunk + 1) * 2 * HD)
        kv[chunk, own:span, : 2 * HD] = (
            k_base[:, cols].astype(f32) + dot(lowk_t, b_key[:, cols], 0, 0)
        ).astype(bf16)
        kv[chunk, own:span, 2 * HD :] = (
            v_base[:, cols].astype(f32) + dot(lowv_t, b_value[:, cols], 0, 0)
        ).astype(bf16)

    for hop in range(1, HOPS + 1):
        @pl.when(seq < hop)
        def _():
            start = (HOPS - hop) * tok
            for chunk in range(chunks):
                kv[chunk, start : start + tok, :] = jnp.zeros((tok, 4 * HD), bf16)
            lows[HOPS - hop] = jnp.zeros(lows.shape[1:], bf16)

        @pl.when(seq + hop >= n_seq)
        def _():
            u_came[hop - 1] = jnp.zeros(u_came.shape[1:], f32)

    pl.semaphore_wait(barrier, len(offsets) + n_dp - 1)

    def slot(chunk, hop):
        start = (HOPS - hop) * tok
        if not isinstance(start, int):
            start = pl.multiple_of(start, tok)
        return kv.at[chunk, pl.ds(start, tok), :]

    near_hop = 1 + 2 * core
    relay_hop = 3 - 2 * core

    def send_two(chunk):
        return remote(
            slot(chunk, 0), slot(chunk, 2), kv_send.at[chunk, 0], kv_recv.at[chunk, 1],
            seq=lax.rem(seq + 2, n_seq),
        )

    def send_near(chunk):
        return remote(
            slot(chunk, 0), slot(chunk, near_hop), kv_send.at[chunk, 1],
            kv_recv.at[chunk, near_hop - 1], seq=lax.rem(seq + near_hop, n_seq),
        )

    def relay(chunk):
        return remote(
            slot(chunk, 2), slot(chunk, relay_hop), relay_send.at[chunk],
            kv_recv.at[chunk, relay_hop - 1], seq=sibling,
        )

    def arrival(chunk, hop):
        return remote(
            slot(chunk, 0), slot(chunk, hop), relay_send.at[chunk], kv_recv.at[chunk, hop - 1],
            seq=sibling,
        )

    def send_low(hop):
        return remote(
            lows.at[HOPS], lows.at[HOPS - hop], low_send.at[hop - 1], low_recv.at[hop - 1],
            seq=lax.rem(seq + hop, n_seq),
        )

    def send_u(hop):
        return remote(
            ukv.at[HOPS - hop], u_came.at[hop - 1], u_send.at[hop - 1], u_recv.at[hop - 1],
            seq=lax.rem(seq - hop + n_seq, n_seq),
        )

    for chunk in range(chunks):
        @pl.when(seq + 2 < n_seq)
        def _():
            send_two(chunk).start()

        @pl.when(seq + near_hop < n_seq)
        def _():
            send_near(chunk).start()

        if chunk == 0:
            for hop in range(1, HOPS + 1):
                @pl.when(seq + hop < n_seq)
                def _():
                    send_low(hop).start()

    length = length_ref[0]
    place = seq * tok + lax.broadcasted_iota(jnp.int32, (tok, 1), 0)
    live = place < length
    for group in range(groups):
        cols = slice(group * 2 * HD, (group + 1) * 2 * HD)
        query = (q_base[:, cols].astype(f32) + dot(lowq_t, b_query[:, cols], 0, 0)).astype(bf16)
        grad = jnp.where(live, d_attn[:, cols].astype(f32), 0.0).astype(bf16)
        for side in range(2):
            part = slice(side * HD, (side + 1) * HD)
            qs[group, side * tok : (side + 1) * tok, :] = query[:, part]
            ds[group, side * tok : (side + 1) * tok, :] = grad[:, part]
            at = slice((2 * group + side) * HD, (2 * group + side + 1) * HD)
            b2q[2 * group + side, :, :HD] = b_query[:, at]
            b2q[2 * group + side, :, HD:] = b_query[:, at]
        at = slice(group * HD, (group + 1) * HD)
        for twice, single in ((b2k, b_key), (b2v, b_value)):
            twice[group, :, :HD] = single[:, at]
            twice[group, :, HD:] = single[:, at]
    key_place = (seq - HOPS) * tok + lax.broadcasted_iota(jnp.int32, (tok, span), 1)
    query_place = seq * tok + lax.broadcasted_iota(jnp.int32, (tok, span), 0)
    distance = query_place - key_place
    allowed = (
        (key_place >= 0)
        & (distance >= 0)
        & (distance <= WINDOW)
        & ((key_place < length) | (distance == 0))
    )
    bias[...] = jnp.where(allowed, 0.0, mask_fill)
    uq[...] = jnp.zeros_like(uq)
    ukv[...] = jnp.zeros_like(ukv)

    tiles_a = width // LANES
    heads = 2 * groups
    at_bq = 3 * tiles_a
    at_bk = at_bq + heads
    at_bv = at_bk + groups
    tiles = at_bv + groups
    if tiles < gsum.shape[0]:
        gsum[tiles:] = jnp.zeros((gsum.shape[0] - tiles, rank, LANES), f32)

    for hop in range(1, HOPS + 1):
        @pl.when(seq >= hop)
        def _():
            remote(
                lows.at[HOPS], lows.at[HOPS - hop], low_send.at[hop - 1], low_recv.at[hop - 1],
                seq=sibling,
            ).wait_recv()
    low_span = jnp.concatenate([lows[index] for index in range(HOPS + 1)], 1)
    lowk2 = jnp.concatenate([low_span[:rank], low_span[:rank]], 1)
    lowv2 = jnp.concatenate([low_span[rank:], low_span[rank:]], 1)
    lowq2 = jnp.concatenate([lowq_t, lowq_t], 1)

    def head(chunk, side):
        group = 2 * chunk + side
        keys = kv[chunk, :, side * HD : (side + 1) * HD]
        values = kv[chunk, :, (2 + side) * HD : (3 + side) * HD]
        query = qs[group]
        d_out = ds[group]
        scores = dot(query, keys, 1, 1) * attn_scale
        scores = (scores.reshape(2, tok, span) + bias[...][None]).reshape(2 * tok, span)
        top = jnp.max(scores, axis=-1, keepdims=True)
        raw = jnp.exp(scores - top)
        probs = raw * (1.0 / jnp.sum(raw, axis=-1, keepdims=True))
        probs_low = probs.astype(bf16)
        output = dot(probs_low, values, 1, 0)
        dprob = dot(d_out, values, 1, 1)
        delta = jnp.sum(probs * dprob, axis=-1, keepdims=True)
        dscore = (probs * (dprob - delta)).astype(bf16)
        d_query = dot(dscore, keys, 1, 0) * attn_scale
        d_key = dot(query, dscore, 0, 0) * attn_scale
        d_value = dot(d_out, probs_low, 0, 0)
        for grad, low2, twice, at, base in (
            (d_key, lowk2, b2k, at_bk, 0),
            (d_value, lowv2, b2v, at_bv, rank),
        ):
            high, rest = halves(grad)
            up = dot(twice[group], jnp.concatenate([high, rest], 0), 1, 0)
            for index in range(HOPS + 1):
                ukv[index, base : base + rank, :] += up[:, index * tok : (index + 1) * tok]
            gsum[at + group] = dot(low2, jnp.concatenate([high, rest], 1), 1, 1)
        high, rest = halves(d_query)
        total = uq[...]
        for part in range(2):
            at = slice(part * tok, (part + 1) * tok)
            number = 2 * group + part
            total += dot(b2q[number], jnp.concatenate([high[at], rest[at]], 1), 1, 1)
            gsum[at_bq + number] = dot(lowq2, jnp.concatenate([high[at], rest[at]], 0), 1, 0)
            kept = jnp.where(live, output[at], 0.0).astype(bf16)
            attention[:, pl.ds(pl.multiple_of(number * HD, HD), HD)] = kept
        uq[...] = total

    @pl.when(chip >= 1)
    def _():
        arrival(0, 2).wait_recv()
        relay(0).start()

    def step(chunk, carry):
        for hop in (1, 3):
            @pl.when(seq >= hop)
            def _():
                arrival(chunk, hop).wait_recv()

        head(chunk, 0)

        @pl.when((chip >= 1) & (chunk + 1 < chunks))
        def _():
            later = lax.rem(chunk + 1, chunks)
            arrival(later, 2).wait_recv()
            relay(later).start()

        head(chunk, 1)
        return carry

    lax.fori_loop(0, chunks, step, 0)

    for hop in range(1, HOPS + 1):
        @pl.when(seq >= hop)
        def _():
            send_u(hop).start()

    grad = dot(uq[...].astype(bf16), rows[...], 1, 0)
    for tile in range(tiles_a):
        gsum[tile] = grad[:, tile * LANES : (tile + 1) * LANES]
    for hop in range(1, HOPS + 1):
        @pl.when(seq + hop < n_seq)
        def _():
            remote(
                ukv.at[HOPS - hop], u_came.at[hop - 1], u_send.at[hop - 1], u_recv.at[hop - 1],
                seq=sibling,
            ).wait_recv()
    pair = ukv[HOPS] + u_came[0] + u_came[1] + u_came[2]
    grad = dot(pair.astype(bf16), rows[...], 1, 0)
    for tile in range(tiles_a):
        at = slice(tile * LANES, (tile + 1) * LANES)
        gsum[tiles_a + tile] = grad[:rank, at]
        gsum[2 * tiles_a + tile] = grad[rank:, at]

    per_chip = n_dp * per_piece
    half = n_chip * per_chip

    def ordered(index):
        return lax.rem(chip + index, n_chip)

    def core_copy(index):
        at = ordered(index) * per_chip
        return remote(
            gsum.at[pl.ds((1 - core) * half + at, per_chip)],
            core_in.at[pl.ds(at, per_chip)],
            s1_send.at[index], s1_recv.at[index], seq=sibling,
        )

    def chip_copy(index):
        return remote(
            chip_out.at[index - 1], chip_in.at[index - 1], s2_send.at[index - 1],
            s2_recv.at[index - 1], seq=2 * ordered(index) + core,
        )

    def dp_copy(index):
        other = lax.rem(dp + index, n_dp)
        return remote(
            dp_out.at[pl.ds(other * per_piece, per_piece)], dp_in.at[index - 1],
            s3_send.at[index - 1], s3_recv.at[index - 1], dp=other,
        )

    order = list(range(1, n_chip)) + [0]
    for index in order:
        core_copy(index).start()
    for index in order:
        core_copy(index).wait_recv()
        at = ordered(index) * per_chip
        both = gsum[pl.ds(core * half + at, per_chip)] + core_in[pl.ds(at, per_chip)]
        if index > 0:
            chip_out[index - 1] = both.astype(bf16)
            chip_copy(index).start()
    for index in range(1, n_chip):
        chip_copy(index).wait_recv()
        both += chip_in[index - 1].astype(f32)
    dp_out[...] = both.astype(bf16)
    core_in[pl.ds(0, per_chip)] = both
    for index in range(1, n_dp):
        dp_copy(index).start()
    piece = core_in[pl.ds(dp * per_piece, per_piece)]
    for index in range(1, n_dp):
        dp_copy(index).wait_recv()
        piece += dp_in[index - 1].astype(f32)

    mine = core * half + chip * per_chip
    final[pl.ds(mine + dp * per_piece, per_piece)] = piece.astype(bf16)

    def dp_share(index, start):
        at = final.at[pl.ds(mine + start * per_piece, per_piece)]
        return remote(
            at, at, s4_send.at[index - 1], s4_recv.at[index - 1], dp=lax.rem(dp + index, n_dp)
        )

    def chip_share(index, start):
        at = final.at[pl.ds(core * half + start * per_chip, per_chip)]
        return remote(
            at, at, s5_send.at[index - 1], s5_recv.at[index - 1], seq=2 * ordered(index) + core
        )

    def core_share(index, side):
        at = final.at[
            pl.ds(side * half + lax.rem(chip - index + n_chip, n_chip) * per_chip, per_chip)
        ]
        return remote(at, at, s6_send.at[index], s6_recv.at[index], seq=sibling)

    for index in range(1, n_dp):
        dp_share(index, dp).start()
    for index in range(1, n_dp):
        dp_share(index, lax.rem(dp - index + n_dp, n_dp)).wait_recv()
    for index in range(1, n_chip):
        chip_share(index, chip).start()
    core_share(0, core).start()
    for index in range(1, n_chip):
        chip_share(index, lax.rem(chip - index + n_chip, n_chip)).wait_recv()
        core_share(index, core).start()
    for index in range(n_chip):
        core_share(index, 1 - core).wait_recv()

    for out, start in (
        (out_aq, 0),
        (out_ak, tiles_a),
        (out_av, 2 * tiles_a),
        (out_bq, at_bq),
        (out_bk, at_bk),
        (out_bv, at_bv),
    ):
        for tile in range(out.shape[1] // LANES):
            out[:, tile * LANES : (tile + 1) * LANES] = final[start + tile].astype(f32)

    for chunk in range(chunks):
        @pl.when(seq + 2 < n_seq)
        def _():
            send_two(chunk).wait_send()

        @pl.when(seq + near_hop < n_seq)
        def _():
            send_near(chunk).wait_send()

        @pl.when(chip >= 1)
        def _():
            relay(chunk).wait_send()

    for hop in range(1, HOPS + 1):
        @pl.when(seq + hop < n_seq)
        def _():
            send_low(hop).wait_send()

        @pl.when(seq >= hop)
        def _():
            send_u(hop).wait_send()

    for index in range(n_chip):
        core_copy(index).wait_send()
        core_share(index, core).wait_send()
    for index in range(1, n_chip):
        chip_copy(index).wait_send()
        chip_share(index, chip).wait_send()
    for index in range(1, n_dp):
        dp_copy(index).wait_send()
        dp_share(index, dp).wait_send()


def shards(
    n_seq,
    n_dp,
    normed_input,
    q_base,
    k_base,
    v_base,
    d_attn,
    lengths,
    a_query,
    b_query,
    a_key,
    b_key,
    a_value,
    b_value,
):
    tok, width = normed_input.shape[1:]
    rank = a_query.shape[1]
    q_cols = q_base.shape[2]
    kv_cols = k_base.shape[2]
    groups = kv_cols // HD
    n_chip = n_seq // 2
    span = (HOPS + 1) * tok
    tiles = (3 * width + q_cols + 2 * kv_cols) // LANES
    pieces = n_seq * n_dp
    per_piece = -(-tiles // pieces)
    total = pieces * per_piece
    per_chip = n_dp * per_piece
    half = n_chip * per_chip
    tile = (rank, LANES)
    vmem = pl.BlockSpec(memory_space=pltpu.VMEM)
    dma = pltpu.SemaphoreType.DMA
    flops = 20 * tok * span * q_cols
    outs = pl.pallas_call(
        functools.partial(kernel, n_seq, n_dp, per_piece),
        out_shape=(
            jax.ShapeDtypeStruct((tok, q_cols), bf16),
            jax.ShapeDtypeStruct((rank, width), f32),
            jax.ShapeDtypeStruct((rank, q_cols), f32),
            jax.ShapeDtypeStruct((rank, width), f32),
            jax.ShapeDtypeStruct((rank, kv_cols), f32),
            jax.ShapeDtypeStruct((rank, width), f32),
            jax.ShapeDtypeStruct((rank, kv_cols), f32),
        ),
        in_specs=[vmem] * 5 + [pl.BlockSpec(memory_space=pltpu.SMEM)] + [vmem] * 6,
        out_specs=(vmem,) * 7,
        scratch_shapes=[
            pltpu.VMEM((groups, 2 * tok, HD), bf16),
            pltpu.VMEM((groups, 2 * tok, HD), bf16),
            pltpu.VMEM((groups // 2, span, 4 * HD), bf16),
            pltpu.VMEM((HOPS + 1, 2 * rank, tok), bf16),
            pltpu.VMEM((tok, span), f32),
            pltpu.VMEM((2 * groups, rank, 2 * HD), bf16),
            pltpu.VMEM((groups, rank, 2 * HD), bf16),
            pltpu.VMEM((groups, rank, 2 * HD), bf16),
            pltpu.VMEM((rank, tok), f32),
            pltpu.VMEM((HOPS + 1, 2 * rank, tok), f32),
            pltpu.VMEM((HOPS, 2 * rank, tok), f32),
            pltpu.VMEM((total,) + tile, f32),
            pltpu.VMEM((half,) + tile, f32),
            pltpu.VMEM((n_chip - 1, per_chip) + tile, bf16),
            pltpu.VMEM((n_chip - 1, per_chip) + tile, bf16),
            pltpu.VMEM((per_chip,) + tile, bf16),
            pltpu.VMEM((n_dp - 1, per_piece) + tile, bf16),
            pltpu.VMEM((total,) + tile, bf16),
            dma((groups // 2, 2)),
            dma((groups // 2, HOPS)),
            dma((groups // 2,)),
            dma((HOPS,)),
            dma((HOPS,)),
            dma((HOPS,)),
            dma((HOPS,)),
            dma((n_chip,)),
            dma((n_chip,)),
            dma((n_chip - 1,)),
            dma((n_chip - 1,)),
            dma((n_dp - 1,)),
            dma((n_dp - 1,)),
            dma((n_dp - 1,)),
            dma((n_dp - 1,)),
            dma((n_chip - 1,)),
            dma((n_chip - 1,)),
            dma((n_chip,)),
            dma((n_chip,)),
        ],
        compiler_params=pltpu.CompilerParams(
            collective_id=0, has_side_effects=True, vmem_limit_bytes=48 * 1024 * 1024
        ),
        cost_estimate=pl.CostEstimate(
            flops=flops, bytes_accessed=6 * 1024 * 1024, transcendentals=span * q_cols
        ),
    )(
        normed_input[0],
        q_base[0],
        k_base[0],
        v_base[0],
        d_attn[0],
        lengths,
        a_query.T,
        a_key.T,
        a_value.T,
        b_query,
        b_key,
        b_value,
    )
    return (outs[0][None], outs[1].T, outs[2], outs[3].T, outs[4], outs[5].T, outs[6])


def solution(mesh):
    return jax.shard_map(
        functools.partial(shards, mesh.shape["seq"], mesh.shape["dp"]),
        mesh=mesh,
        in_specs=(
            P("dp", "seq", None),
            P("dp", "seq", None),
            P("dp", "seq", None),
            P("dp", "seq", None),
            P("dp", "seq", None),
            P("dp"),
            P(),
            P(),
            P(),
            P(),
            P(),
            P(),
        ),
        out_specs=(P("dp", "seq", None), P(), P(), P(), P(), P(), P()),
        check_vma=False,
    )
```
